32 devices in a mesh: dp: 8 (over z, y), mp: 4 (over x, core).
Axes of the slice: x: 2, y: 2, z: 4, core: 2. Of those that a mesh axis runs over, the one named last changes fastest.
Arguments:
- points: float32 [16384, 256], P('dp'), may hold values from -28 to 28
- residual: float32 [128, 16384], P('mp', 'dp'), may hold values from -6 to 6
- coeffs: float32 [128, 16384], P('mp', 'dp'), may hold values from -4 to 4
- block_index: int32 [512], replicated, may hold values from 0 to 16383, as said below
Outputs:
- new_residual: float32 [128, 16384], P('mp', 'dp')
- new_coeffs: float32 [128, 16384], P('mp', 'dp')
The draws below stay inside these ranges and needn't reach their ends.
Inputs may be any that keep to these rules, and one draw needn't show every extreme that they name: `block_index`: distinct example indices; the 2048 examples of one index of dp hold at most 256 of them, and those of some index hold exactly 256.
All inputs are finite; a program needn't handle non-finite values.
Results may differ from the reference program's by a relative error of at most 0.00018.
Values sent between devices are 32-bit elements; how exact they have to be, the bound alone decides.
A program may use at most 64 MiB of HBM per device.

```python
import math
import jax
import jax.numpy as jnp
from jax import lax

FEAT = 256
OUTPUTS = 128
BLOCK = 512
ROWS = 2048
EXAMPLES = 16384
MOST = 256


def draw_points(key, part):
    base_key, scale_key = jax.random.split(key, 2)
    position = jnp.arange(EXAMPLES, dtype=jnp.float32) / EXAMPLES
    rising = 1.0 + 2.0 * position
    spread = jnp.exp(jax.random.uniform(scale_key, (EXAMPLES, 1), jnp.float32) * math.log(10.0))
    scale = jnp.sqrt(rising[:, None] * spread)
    base = jax.random.truncated_normal(base_key, -5.0, 5.0, (EXAMPLES, FEAT), jnp.float32)
    return (base * scale).astype(jnp.float32)


def draw_block_index(key, part):
    subkeys = jax.random.split(key, 4)
    shard_count = EXAMPLES // ROWS
    others = shard_count - 1
    coordinate = jnp.arange(BLOCK, dtype=jnp.int32)
    remaining = coordinate - MOST
    order_pos = jnp.where(coordinate < MOST, 0, 1 + remaining % others)
    slot_rank = jnp.where(coordinate < MOST, coordinate, remaining // others)
    shuffle = jax.random.permutation(subkeys[0], shard_count).astype(jnp.int32)
    shard_of = shuffle[order_pos]
    offset = jax.random.randint(subkeys[1], (shard_count,), 0, ROWS)
    stride = 2 * jax.random.randint(subkeys[2], (shard_count,), 0, ROWS // 2) + 1
    row_within = (offset[shard_of] + slot_rank * stride[shard_of]) % ROWS
    chosen = shard_of * ROWS + row_within
    reorder = jax.random.permutation(subkeys[3], BLOCK).astype(jnp.int32)
    return chosen[reorder].astype(jnp.int32)


def block_scale(own_key, shape, pieces, low, high):
    def one(dim, shards_of):
        heights = jax.random.uniform(jax.random.fold_in(jax.random.fold_in(own_key, 6), dim), (shards_of,), jnp.float32, low / len(pieces), high / len(pieces))
        return jnp.repeat(jnp.exp(heights), shape[dim] // shards_of).reshape((-1,) + (1,) * (len(shape) - dim - 1))

    loudness = one(*pieces[0])
    for cut in pieces[1:]:
        loudness = loudness * one(*cut)
    return loudness


def centred(stream_key, shape, width, reach, cuts=(), held_as=jnp.bfloat16):
    result = jax.random.normal(stream_key, shape, jnp.float32) * width
    if len(cuts) > 0:
        result = block_scale(stream_key, shape, cuts, -0.22, 0.18) * result
    return jnp.clip(result, min=-reach, max=reach).astype(held_as)


def setup_inputs(seed: int = 0) -> dict:
    key_list = jax.random.split(jax.random.key(seed), 5)
    points = draw_points(jax.random.fold_in(key_list[4], 71), 0)
    residual = centred(key_list[1], (OUTPUTS, EXAMPLES), 1.0, 6.0, ((0, 4), (1, 8)), jnp.float32)
    coeffs = centred(key_list[2], (OUTPUTS, EXAMPLES), 0.5, 4.0, ((0, 4), (1, 8)), jnp.float32)
    block_index = draw_block_index(jax.random.fold_in(key_list[4], 71), 0)
    return {"points": points, "residual": residual, "coeffs": coeffs, "block_index": block_index}


ridge_weight = 1.0

def reference(points, residual, coeffs, block_index):
    highest = lax.Precision.HIGHEST
    mean_sq = jnp.sum(points * points) / EXAMPLES
    block_points = points[block_index]
    block_resid = residual[:, block_index]
    block_sq = jnp.sum(block_points * block_points, axis=1)
    inner_block = lax.dot_general(block_points.astype(jnp.float32), block_points.astype(jnp.float32), (((1,), (1,)), ((), ())), precision=highest, preferred_element_type=jnp.float32)
    kernel_block = jnp.exp(-(block_sq[:, None] + block_sq[None, :] - 2.0 * inner_block) / mean_sq)
    system = kernel_block + ridge_weight * jnp.eye(BLOCK, dtype=jnp.float32)
    factor = jnp.linalg.cholesky(system)
    increment = jax.scipy.linalg.cho_solve((factor, True), block_resid.T).T
    shard_count = EXAMPLES // ROWS
    grouped = points.reshape(shard_count, ROWS, FEAT)

    def change_of(group):
        group_sq = jnp.sum(group * group, axis=1)
        inner = lax.dot_general(block_points.astype(jnp.float32), group.astype(jnp.float32), (((1,), (1,)), ((), ())), precision=highest, preferred_element_type=jnp.float32)
        weights = jnp.exp(-(block_sq[:, None] + group_sq[None, :] - 2.0 * inner) / mean_sq)
        return jnp.dot(increment.astype(jnp.float32), weights.astype(jnp.float32), precision=highest, preferred_element_type=jnp.float32)
    changes = lax.map(change_of, grouped)
    change = jnp.transpose(changes, (1, 0, 2)).reshape(OUTPUTS, EXAMPLES)
    new_residual = (residual - change).at[:, block_index].add(-ridge_weight * increment)
    new_coeffs = coeffs.at[:, block_index].add(increment)
    return (new_residual, new_coeffs)
```

```python
import functools

import jax
import jax.numpy as jnp
from jax import lax
from jax.experimental import pallas as pl
from jax.experimental.pallas import tpu as pltpu
from jax.sharding import PartitionSpec as P

MESH = pl.DeviceIdType.MESH
F32 = jnp.float32
BF16 = jnp.bfloat16
HIGHEST = lax.Precision.HIGHEST
ridge_weight = 1.0
PIVOT = 128
GROUP = 8
VMEM_BYTES = 56 * 1024 * 1024


def pieces(x, count):
    out = []
    for _ in range(count):
        part = x.astype(BF16)
        out.append(part)
        x = x - part.astype(F32)
    return out


def dot(a, b, dims=((1,), (0,)), precision=None):
    return lax.dot_general(a, b, (dims, ((), ())), precision=precision, preferred_element_type=F32)


def dot3(a, b, dims=((1,), (0,))):
    a0, a1 = pieces(a, 2)
    b0, b1 = pieces(b, 2)
    return dot(a0, b0, dims) + (dot(a0, b1, dims) + dot(a1, b0, dims))


def picked_points(index_col, points, base):
    local = index_col - base
    hot = (lax.broadcasted_iota(jnp.int32, (index_col.shape[0], points.shape[0]), 1) == local).astype(BF16)
    total = None
    for part in reversed(pieces(points, 3)):
        term = dot(hot, part)
        total = term if total is None else total + term
    return total


def picked_resid(index_row, residual, base):
    local = index_row - base
    hot = (lax.broadcasted_iota(jnp.int32, (residual.shape[1], index_row.shape[1]), 0) == local).astype(BF16)
    rows = residual.shape[0]
    got = dot(jnp.concatenate(pieces(residual, 3), axis=0), hot)
    return (got[2 * rows :] + got[rows : 2 * rows]) + got[:rows]


def square_sums(points):
    squares = points * points
    sums = jnp.sum(squares.reshape(points.shape[0] // 8, 8, points.shape[1]), axis=0)
    total = sums[:, :128]
    for start in range(128, points.shape[1], 128):
        total = total + sums[:, start : start + 128]
    return total


def exchange_kernel(dp, mp, index_col, index_row, points, residual, out_points, out_resid, out_squares,
                    send, landed, share, full, squares, first_send, first_recv, square_send, square_recv,
                    second_send, second_recv, third_send, third_recv):
    me = lax.axis_index("dp")
    col = lax.axis_index("mp")
    block = index_col.shape[0]
    feat = points.shape[1]
    quarter = block // mp
    rows = quarter // dp
    out_rows = residual.shape[0]
    base = me * points.shape[0]

    barrier = pltpu.get_barrier_semaphore()
    for step in range(1, dp):
        pl.semaphore_signal(barrier, inc=1, device_id=(lax.rem(me + step, dp), col), device_id_type=MESH)
    for step in range(1, mp):
        pl.semaphore_signal(barrier, inc=1, device_id=(me, lax.rem(col + step, mp)), device_id_type=MESH)

    squares[me] = square_sums(points[...])
    got = picked_points(index_col[pl.ds(pl.multiple_of(col * quarter, quarter), quarter), :], points[...], base)
    resid = picked_resid(index_row[...], residual[...], base)
    for d in range(dp):
        send[d, :, :feat] = got[d * rows : (d + 1) * rows]
        tile, start = divmod(d * rows, out_rows)
        send[d, :, feat:] = resid[start : start + rows, tile * 128 : (tile + 1) * 128]
    pl.semaphore_wait(barrier, dp - 1 + mp - 1)

    first, norms = [], []
    for step in range(1, dp):
        peer = lax.rem(me + step, dp)
        first.append(pltpu.make_async_remote_copy(
            src_ref=send.at[peer], dst_ref=landed.at[me], send_sem=first_send.at[step], recv_sem=first_recv.at[step],
            device_id=(peer, col), device_id_type=MESH))
        first[-1].start()
        norms.append(pltpu.make_async_remote_copy(
            src_ref=squares.at[me], dst_ref=squares.at[me], send_sem=square_send.at[step],
            recv_sem=square_recv.at[step], device_id=(peer, col), device_id_type=MESH))
        norms[-1].start()
    landed[me] = send[me]
    for copy in first:
        copy.wait()
    total = landed[0]
    for d in range(1, dp):
        total = total + landed[d]
    share[...] = total
    second = []
    for step in range(1, dp):
        peer = lax.rem(me + step, dp)
        second.append(pltpu.make_async_remote_copy(
            src_ref=share, dst_ref=full.at[me], send_sem=second_send.at[step], recv_sem=second_recv.at[step],
            device_id=(peer, col), device_id_type=MESH))
        second[-1].start()
    full[me] = total
    third = []
    for step in range(dp):
        source = lax.rem(me + dp - step, dp)
        if step > 0:
            second[step - 1].wait_recv()
        place = pl.ds(pl.multiple_of(col * quarter + source * rows, rows), rows)
        out_points[place, :] = full[source, :, :feat]
        for other in range(1, mp):
            third.append(pltpu.make_async_remote_copy(
                src_ref=full.at[source, :, pl.ds(0, feat)], dst_ref=out_points.at[place, :],
                send_sem=third_send.at[step, other], recv_sem=third_recv.at[step, other],
                device_id=(me, lax.rem(col + other, mp)), device_id_type=MESH))
            third[-1].start()
    for copy in norms:
        copy.wait()
    sums = squares[0]
    for d in range(1, dp):
        sums = sums + squares[d]
    out_squares[...] = sums
    for d in range(dp):
        tile, start = divmod(d * rows, out_rows)
        out_resid[start : start + rows, tile * 128 : (tile + 1) * 128] = full[d, :, feat:]
    for copy in second:
        copy.wait_send()
    for copy in third:
        copy.wait()


def exchange(dp, mp, index_col, index_row, points, residual):
    block, feat = index_col.shape[0], points.shape[1]
    rows = block // (dp * mp)
    out_rows = residual.shape[0]
    width = feat + 128
    vmem = pl.BlockSpec(memory_space=pltpu.VMEM)
    dma = pltpu.SemaphoreType.DMA
    return pl.pallas_call(
        functools.partial(exchange_kernel, dp, mp),
        out_shape=(jax.ShapeDtypeStruct((block, feat), F32), jax.ShapeDtypeStruct((out_rows, block), F32),
                   jax.ShapeDtypeStruct((8, 128), F32)),
        in_specs=[vmem] * 4,
        out_specs=(vmem,) * 3,
        scratch_shapes=[
            pltpu.VMEM((dp, rows, width), F32), pltpu.VMEM((dp, rows, width), F32), pltpu.VMEM((rows, width), F32),
            pltpu.VMEM((dp, rows, width), F32), pltpu.VMEM((dp, 8, 128), F32),
            dma((dp,)), dma((dp,)), dma((dp,)), dma((dp,)), dma((dp,)), dma((dp,)), dma((dp, mp)), dma((dp, mp)),
        ],
        compiler_params=pltpu.CompilerParams(collective_id=0, has_side_effects=True, vmem_limit_bytes=VMEM_BYTES),
    )(index_col, index_row, points, residual)


def exchange_by_sums(dp, mp, index_col, index_row, points, residual):
    base = lax.axis_index("dp") * points.shape[0]
    local = index_col[:, 0] - base
    mine = (local >= 0) & (local < points.shape[0])
    safe = jnp.where(mine, local, 0)
    got = jnp.where(mine[:, None], points[safe], 0.0)
    resid = jnp.where(mine[None, :], residual[:, safe], 0.0)
    return tuple(lax.psum(x, "dp") for x in (got, resid, square_sums(points)))


def invert(matrix):
    size = matrix.shape[0]
    lane = lax.broadcasted_iota(jnp.int32, (size, size), 1)
    lane_group = lax.broadcasted_iota(jnp.int32, (GROUP, size), 1)
    row_group = lax.broadcasted_iota(jnp.int32, (GROUP, size), 0)
    for start in range(0, size, GROUP):
        stop = start + GROUP
        columns = [jnp.broadcast_to(matrix[:, j : j + 1], (size, size)) for j in range(start, stop)]
        small = [c[start:stop] for c in columns]
        panel = jnp.where((lane_group >= start) & (lane_group < stop),
                          (lane_group - start == row_group).astype(F32), matrix[start:stop])
        for j in range(GROUP):
            on_row = row_group == j
            scale = 1.0 / small[j][j : j + 1]
            factor = jnp.where(on_row, 0.0, small[j])
            row = panel[j : j + 1] * scale
            panel = jnp.where(on_row, row, panel) - factor * row
            for l in range(j + 1, GROUP):
                entry = small[l][j : j + 1] * scale
                small[l] = jnp.where(on_row, entry, small[l]) - factor * entry
        matrix = jnp.where((lane >= start) & (lane < stop), 0.0, matrix)
        for j in range(GROUP):
            matrix = matrix - columns[j] * panel[j : j + 1]
        parts = [matrix[:start], panel, matrix[stop:]]
        matrix = jnp.concatenate([p for p in parts if p.shape[0]], axis=0)
    return matrix


def step_kernel(examples, index_col, points, residual, coeffs, block_points, block_resid, squares,
                new_residual, new_coeffs, system, inverses, rhs):
    block, feat = block_points.shape
    count = points.shape[0]
    out_rows = residual.shape[0]
    base = lax.axis_index("dp") * count
    mean_sq = jnp.sum(squares[...]) / examples
    ones = jnp.ones((8, feat), F32)
    centers = block_points[...]
    center_sq = jnp.sum(centers * centers, axis=1, keepdims=True)
    center_sq_row = dot(ones, centers * centers, ((1,), (1,)), HIGHEST)[:1]
    inner = dot(centers, centers, ((1,), (1,)), HIGHEST)
    diagonal = lax.broadcasted_iota(jnp.int32, (block, block), 0) == lax.broadcasted_iota(jnp.int32, (block, block), 1)
    system[...] = jnp.exp(-(center_sq + center_sq_row - 2.0 * inner) / mean_sq) + jnp.where(diagonal, ridge_weight, 0.0)
    rhs[...] = block_resid[...]

    for start in range(0, block, PIVOT):
        stop = start + PIVOT
        inverse = invert(system[start:stop, start:stop])
        inverses[start:stop, :] = inverse
        if stop < block:
            right = system[start:stop, stop:]
            scaled = dot(inverse, right, precision=HIGHEST)
            system[stop:, stop:] = system[stop:, stop:] - dot(right, scaled, ((0,), (0,)), HIGHEST)
            rhs[:, stop:] = rhs[:, stop:] - dot(rhs[:, start:stop], scaled, precision=HIGHEST)
    for start in reversed(range(0, block, PIVOT)):
        stop = start + PIVOT
        now = rhs[:, start:stop]
        if stop < block:
            now = now - dot(rhs[:, stop:], system[start:stop, stop:], ((1,), (1,)), HIGHEST)
        rhs[:, start:stop] = dot(now, inverses[start:stop, :], precision=HIGHEST)

    high, mid, low = pieces(rhs[...], 3)
    stack3 = jnp.concatenate([high, mid, low], axis=0)
    stack2 = jnp.concatenate([high, mid], axis=0)
    tile = 256

    @pl.loop(0, count // tile)
    def _(i):
        here = pl.ds(pl.multiple_of(i * tile, tile), tile)
        some = points[here, :]
        some_sq = dot(ones, some * some, ((1,), (1,)), HIGHEST)[:1]
        inner = dot(centers, some, ((1,), (1,)), HIGHEST)
        weights = jnp.exp(-(center_sq + some_sq - 2.0 * inner) / mean_sq)
        w0, w1 = pieces(weights, 2)
        main = dot(stack2, w0)
        change = main[:out_rows] + (main[out_rows:] + dot(high, w1))
        local = index_col[...] - (base + i * tile)
        hot = (lax.broadcasted_iota(jnp.int32, (block, tile), 1) == local).astype(BF16)
        placed = dot(stack3, hot)
        added = (placed[2 * out_rows :] + placed[out_rows : 2 * out_rows]) + placed[:out_rows]
        new_residual[:, here] = (residual[:, here] - change) - ridge_weight * added
        new_coeffs[:, here] = coeffs[:, here] + added


def step(examples, index_col, points, residual, coeffs, block_points, block_resid, squares):
    block = block_points.shape[0]
    vmem = pl.BlockSpec(memory_space=pltpu.VMEM)
    return pl.pallas_call(
        functools.partial(step_kernel, examples),
        out_shape=(jax.ShapeDtypeStruct(residual.shape, F32), jax.ShapeDtypeStruct(coeffs.shape, F32)),
        in_specs=[vmem] * 7,
        out_specs=(vmem,) * 2,
        scratch_shapes=[pltpu.VMEM((block, block), F32), pltpu.VMEM((block, PIVOT), F32),
                        pltpu.VMEM(residual.shape[:1] + (block,), F32)],
        compiler_params=pltpu.CompilerParams(vmem_limit_bytes=VMEM_BYTES),
    )(index_col, points, residual, coeffs, block_points, block_resid, squares)


def solution(mesh):
    dp, mp = mesh.shape["dp"], mesh.shape["mp"]

    def on_device(points, residual, coeffs, block_index):
        index_col, index_row = block_index[:, None], block_index[None, :]
        block, out_rows = block_index.shape[0], residual.shape[0]
        rows = block // (dp * mp)
        fits = rows % 8 == 0 and out_rows % rows == 0 and rows * dp * mp == block and out_rows * block == dp * rows * 128
        gathered = (exchange if fits else exchange_by_sums)(dp, mp, index_col, index_row, points, residual)
        return step(points.shape[0] * dp, index_col, points, residual, coeffs, *gathered)

    return jax.shard_map(
        on_device,
        mesh=mesh,
        in_specs=(P("dp", None), P("mp", "dp"), P("mp", "dp"), P()),
        out_specs=(P("mp", "dp"), P("mp", "dp")),
        check_vma=False,
    )
```

```python
import functools

import jax
import jax.numpy as jnp
from jax import lax
from jax.experimental import pallas as pl
from jax.experimental.pallas import tpu as pltpu
from jax.sharding import PartitionSpec as P

MESH = pl.DeviceIdType.MESH
F32 = jnp.float32
BF16 = jnp.bfloat16
HIGHEST = lax.Precision.HIGHEST
ridge_weight = 1.0
PIVOT = 128
GROUP = 8
VMEM_BYTES = 56 * 1024 * 1024


def pieces(x, count):
    out = []
    for _ in range(count):
        part = x.astype(BF16)
        out.append(part)
        x = x - part.astype(F32)
    return out


def dot(a, b, dims=((1,), (0,)), precision=None):
    return lax.dot_general(a, b, (dims, ((), ())), precision=precision, preferred_element_type=F32)


def dot3(a, b, dims=((1,), (0,))):
    a0, a1 = pieces(a, 2)
    b0, b1 = pieces(b, 2)
    return dot(a0, b0, dims) + (dot(a0, b1, dims) + dot(a1, b0, dims))


def picked_points(index_col, points, base):
    local = index_col - base
    hot = (lax.broadcasted_iota(jnp.int32, (index_col.shape[0], points.shape[0]), 1) == local).astype(BF16)
    total = None
    for part in reversed(pieces(points, 3)):
        term = dot(hot, part)
        total = term if total is None else total + term
    return total


def picked_resid(index_row, residual, base):
    local = index_row - base
    hot = (lax.broadcasted_iota(jnp.int32, (residual.shape[1], index_row.shape[1]), 0) == local).astype(BF16)
    rows = residual.shape[0]
    got = dot(jnp.concatenate(pieces(residual, 3), axis=0), hot)
    return (got[2 * rows :] + got[rows : 2 * rows]) + got[:rows]


def square_sums(points):
    squares = points * points
    sums = jnp.sum(squares.reshape(points.shape[0] // 8, 8, points.shape[1]), axis=0)
    total = sums[:, :128]
    for start in range(128, points.shape[1], 128):
        total = total + sums[:, start : start + 128]
    return total


def exchange_kernel(dp, mp, index_row, points, residual, out_points, out_resid, out_squares,
                    send, landed, share, full, squares, first_send, first_recv, square_send, square_recv,
                    second_send, second_recv, third_send, third_recv):
    me = lax.axis_index("dp")
    col = lax.axis_index("mp")
    block = index_row.shape[1]
    feat = points.shape[1]
    quarter = block // mp
    rows = quarter // dp
    out_rows = residual.shape[0]
    base = me * points.shape[0]

    barrier = pltpu.get_barrier_semaphore()
    for step in range(1, dp):
        pl.semaphore_signal(barrier, inc=1, device_id=(lax.rem(me + step, dp), col), device_id_type=MESH)
    near, far = col + 1 - 2 * lax.rem(col, 2), lax.rem(col + 2, mp)
    for other in (near, far):
        pl.semaphore_signal(barrier, inc=1, device_id=(me, other), device_id_type=MESH)

    squares[me] = square_sums(points[...])
    own = index_row[:, pl.ds(pl.multiple_of(col * quarter, quarter), quarter)]
    own = jnp.transpose(jnp.broadcast_to(own, (128, quarter)))[:, :1]
    got = picked_points(own, points[...], base)
    resid = picked_resid(index_row[...], residual[...], base)
    for d in range(dp):
        send[d, :, :feat] = got[d * rows : (d + 1) * rows]
        tile, start = divmod(d * rows, out_rows)
        send[d, :, feat:] = resid[start : start + rows, tile * 128 : (tile + 1) * 128]
    pl.semaphore_wait(barrier, dp - 1 + 2)

    first, norms = [], []
    for step in range(1, dp):
        peer = lax.rem(me + step, dp)
        first.append(pltpu.make_async_remote_copy(
            src_ref=send.at[peer], dst_ref=landed.at[me], send_sem=first_send.at[step], recv_sem=first_recv.at[step],
            device_id=(peer, col), device_id_type=MESH))
        first[-1].start()
        norms.append(pltpu.make_async_remote_copy(
            src_ref=squares.at[me], dst_ref=squares.at[me], send_sem=square_send.at[step],
            recv_sem=square_recv.at[step], device_id=(peer, col), device_id_type=MESH))
        norms[-1].start()
    landed[me] = send[me]
    for copy in first:
        copy.wait()
    total = landed[0]
    for d in range(1, dp):
        total = total + landed[d]
    share[...] = total
    second = []
    for step in range(1, dp):
        peer = lax.rem(me + step, dp)
        second.append(pltpu.make_async_remote_copy(
            src_ref=share, dst_ref=full.at[me], send_sem=second_send.at[step], recv_sem=second_recv.at[step],
            device_id=(peer, col), device_id_type=MESH))
        second[-1].start()
    full[me] = total
    third = []
    for step in range(dp):
        source = lax.rem(me + dp - step, dp)
        if step > 0:
            second[step - 1].wait_recv()
        place = pl.ds(pl.multiple_of(col * quarter + source * rows, rows), rows)
        out_points[place, :] = full[source, :, :feat]
        for kind, other in enumerate((far, near)):
            third.append(pltpu.make_async_remote_copy(
                src_ref=full.at[source, :, pl.ds(0, feat)], dst_ref=out_points.at[place, :],
                send_sem=third_send.at[step, kind], recv_sem=third_recv.at[step, kind],
                device_id=(me, other), device_id_type=MESH))
            third[-1].start()
    fourth = []
    for step in range(dp):
        source = lax.rem(me + dp - step, dp)
        third[2 * step].wait_recv()
        place = pl.ds(pl.multiple_of(far * quarter + source * rows, rows), rows)
        fourth.append(pltpu.make_async_remote_copy(
            src_ref=out_points.at[place, :], dst_ref=out_points.at[place, :],
            send_sem=third_send.at[step, 2], recv_sem=third_recv.at[step, 2],
            device_id=(me, near), device_id_type=MESH))
        fourth[-1].start()
    for copy in norms:
        copy.wait()
    sums = squares[0]
    for d in range(1, dp):
        sums = sums + squares[d]
    out_squares[...] = sums
    for d in range(dp):
        tile, start = divmod(d * rows, out_rows)
        out_resid[start : start + rows, tile * 128 : (tile + 1) * 128] = full[d, :, feat:]
    for copy in second:
        copy.wait_send()
    for step in range(dp):
        third[2 * step].wait_send()
        third[2 * step + 1].wait()
        fourth[step].wait()


def exchange(dp, mp, index_row, points, residual):
    block, feat = index_row.shape[1], points.shape[1]
    rows = block // (dp * mp)
    out_rows = residual.shape[0]
    width = feat + 128
    vmem = pl.BlockSpec(memory_space=pltpu.VMEM)
    dma = pltpu.SemaphoreType.DMA
    return pl.pallas_call(
        functools.partial(exchange_kernel, dp, mp),
        out_shape=(jax.ShapeDtypeStruct((block, feat), F32), jax.ShapeDtypeStruct((out_rows, block), F32),
                   jax.ShapeDtypeStruct((8, 128), F32)),
        in_specs=[vmem] * 3,
        out_specs=(vmem,) * 3,
        scratch_shapes=[
            pltpu.VMEM((dp, rows, width), F32), pltpu.VMEM((dp, rows, width), F32), pltpu.VMEM((rows, width), F32),
            pltpu.VMEM((dp, rows, width), F32), pltpu.VMEM((dp, 8, 128), F32),
            dma((dp,)), dma((dp,)), dma((dp,)), dma((dp,)), dma((dp,)), dma((dp,)), dma((dp, 3)), dma((dp, 3)),
        ],
        compiler_params=pltpu.CompilerParams(collective_id=0, has_side_effects=True, vmem_limit_bytes=VMEM_BYTES),
    )(index_row, points, residual)


def exchange_by_sums(dp, mp, index_row, points, residual):
    base = lax.axis_index("dp") * points.shape[0]
    local = index_row[0] - base
    mine = (local >= 0) & (local < points.shape[0])
    safe = jnp.where(mine, local, 0)
    got = jnp.where(mine[:, None], points[safe], 0.0)
    resid = jnp.where(mine[None, :], residual[:, safe], 0.0)
    return tuple(lax.psum(x, "dp") for x in (got, resid, square_sums(points)))


def invert(matrix, beside):
    size = matrix.shape[0]
    lane = lax.broadcasted_iota(jnp.int32, (size, size), 1)
    lane_group = lax.broadcasted_iota(jnp.int32, (GROUP, size), 1)
    row_group = lax.broadcasted_iota(jnp.int32, (GROUP, size), 0)
    for start in range(0, size, GROUP):
        stop = start + GROUP
        columns = [jnp.broadcast_to(matrix[:, j : j + 1], (size, size)) for j in range(start, stop)]
        small = [c[start:stop] for c in columns]
        panel = jnp.where((lane_group >= start) & (lane_group < stop),
                          (lane_group - start == row_group).astype(F32), matrix[start:stop])
        for j in range(0, GROUP, 2):
            k = j + 1
            on_j, on_k = row_group == j, row_group == k
            p, q, r = small[j][j : j + 1], small[j][k : k + 1], small[k][k : k + 1]
            scale = 1.0 / (p * r - q * q)
            low, cross, high = r * scale, q * scale, p * scale
            left = jnp.where(on_j, -1.0, jnp.where(on_k, 0.0, small[j]))
            right = jnp.where(on_k, -1.0, jnp.where(on_j, 0.0, small[k]))
            pivots = on_j | on_k

            def reduced(x):
                x0, x1 = x[j : j + 1], x[k : k + 1]
                y0, y1 = x0 * low - x1 * cross, x1 * high - x0 * cross
                return jnp.where(pivots, 0.0, x) - left * y0 - right * y1

            for l in range(j + 2, GROUP):
                small[l] = reduced(small[l])
            panel = reduced(panel)
        beside(start // GROUP)
        matrix = jnp.where((lane >= start) & (lane < stop), 0.0, matrix)
        for j in range(GROUP):
            matrix = matrix - columns[j] * panel[j : j + 1]
        parts = [matrix[:start], panel, matrix[stop:]]
        matrix = jnp.concatenate([p for p in parts if p.shape[0]], axis=0)
    return matrix


def step_kernel(examples, index_row, points, residual, coeffs, block_points, block_resid, squares,
                new_residual, new_coeffs, system, weights0, weights1, index_col):
    block, feat = block_points.shape
    count = points.shape[0]
    out_rows = residual.shape[0]
    base = lax.axis_index("dp") * count
    inverse_mean = examples / jnp.sum(squares[...])
    ones = jnp.ones((8, feat), F32)
    centers = block_points[...]
    center_sq = jnp.sum(centers * centers, axis=1, keepdims=True)
    center_sq_row = dot(ones, centers * centers, ((1,), (1,)), HIGHEST)[:1]
    inner = dot(centers, centers, ((1,), (1,)), HIGHEST)
    diagonal = lax.broadcasted_iota(jnp.int32, (block, block), 0) == lax.broadcasted_iota(jnp.int32, (block, block), 1)
    system[:block, :] = (jnp.exp(-(center_sq + center_sq_row - 2.0 * inner) * inverse_mean)
                         + jnp.where(diagonal, ridge_weight, 0.0))
    system[block:, :] = block_resid[...]
    index_col[...] = jnp.transpose(jnp.broadcast_to(index_row[...], (128, block)))

    groups = PIVOT // GROUP
    strips = block // PIVOT
    some_rows = count // (strips * (groups // strips))
    lane = lax.broadcasted_iota(jnp.int32, (PIVOT, block), 1)
    lane_all = lax.broadcasted_iota(jnp.int32, (block + out_rows, block), 1)

    @pl.loop(0, strips)
    def _(step):
        here = pl.ds(pl.multiple_of(step * PIVOT, PIVOT), PIVOT)
        held = {}

        def beside(n):
            strip = n % strips
            first = step * (groups // strips) + n // strips
            there = pl.ds(pl.multiple_of(first * some_rows, some_rows), some_rows)
            some = points[there, :]
            if strip == 0:
                held["sq"] = dot(ones, some * some, ((1,), (1,)), HIGHEST)[:1]
            rows = slice(strip * PIVOT, (strip + 1) * PIVOT)
            inner = dot(block_points[rows, :], some, ((1,), (1,)), HIGHEST)
            weights = jnp.exp(-(center_sq[rows] + held["sq"] - 2.0 * inner) * inverse_mean)
            w0, w1 = pieces(weights, 2)
            weights0[rows, there] = w0
            weights1[rows, there] = w1

        inverse = invert(system[here, here], beside)
        inside = (lane >= step * PIVOT) & (lane < (step + 1) * PIVOT)
        scaled = dot(inverse, system[here, :], precision=HIGHEST)
        scaled = jnp.where(inside, -jnp.concatenate([inverse] * strips, axis=1), scaled)
        left = system[:, here]
        inside_all = (lane_all >= step * PIVOT) & (lane_all < (step + 1) * PIVOT)
        system[...] = jnp.where(inside_all, 0.0, system[...]) - dot(left, scaled, precision=HIGHEST)

    high, mid, low = pieces(system[block:, :], 3)
    stack3 = jnp.concatenate([high, mid, low], axis=0)
    stack2 = jnp.concatenate([high, mid], axis=0)
    tile = 512

    @pl.loop(0, count // tile)
    def _(i):
        here = pl.ds(pl.multiple_of(i * tile, tile), tile)
        main = dot(stack2, weights0[:, here])
        change = main[:out_rows] + (main[out_rows:] + dot(high, weights1[:, here]))
        local = jnp.concatenate([index_col[...]] * (tile // 128), axis=1) - (base + i * tile)
        hot = (lax.broadcasted_iota(jnp.int32, (block, tile), 1) == local).astype(BF16)
        placed = dot(stack3, hot)
        added = (placed[2 * out_rows :] + placed[out_rows : 2 * out_rows]) + placed[:out_rows]
        new_residual[:, here] = (residual[:, here] - change) - ridge_weight * added
        new_coeffs[:, here] = coeffs[:, here] + added


def step(examples, index_row, points, residual, coeffs, block_points, block_resid, squares):
    block = block_points.shape[0]
    vmem = pl.BlockSpec(memory_space=pltpu.VMEM)
    return pl.pallas_call(
        functools.partial(step_kernel, examples),
        out_shape=(jax.ShapeDtypeStruct(residual.shape, F32), jax.ShapeDtypeStruct(coeffs.shape, F32)),
        in_specs=[vmem] * 7,
        out_specs=(vmem,) * 2,
        scratch_shapes=[pltpu.VMEM((block + residual.shape[0], block), F32),
                        pltpu.VMEM((block, points.shape[0]), BF16), pltpu.VMEM((block, points.shape[0]), BF16),
                        pltpu.VMEM((block, 128), jnp.int32)],
        compiler_params=pltpu.CompilerParams(vmem_limit_bytes=VMEM_BYTES),
    )(index_row, points, residual, coeffs, block_points, block_resid, squares)


def solution(mesh):
    dp, mp = mesh.shape["dp"], mesh.shape["mp"]

    def on_device(points, residual, coeffs, block_index):
        index_row = block_index[None, :]
        block, out_rows = block_index.shape[0], residual.shape[0]
        rows = block // (dp * mp)
        fits = mp == 4 and block // mp == 128 and rows % 8 == 0 and out_rows % rows == 0 and rows * dp * mp == block and out_rows * block == dp * rows * 128
        gathered = (exchange if fits else exchange_by_sums)(dp, mp, index_row, points, residual)
        return step(points.shape[0] * dp, index_row, points, residual, coeffs, *gathered)

    return jax.shard_map(
        on_device,
        mesh=mesh,
        in_specs=(P("dp", None), P("mp", "dp"), P("mp", "dp"), P()),
        out_specs=(P("mp", "dp"), P("mp", "dp")),
        check_vma=False,
    )
```

```python
import functools

import jax
import jax.numpy as jnp
from jax import lax
from jax.experimental import pallas as pl
from jax.experimental.pallas import tpu as pltpu
from jax.sharding import PartitionSpec as P

MESH = pl.DeviceIdType.MESH
F32 = jnp.float32
BF16 = jnp.bfloat16
HIGHEST = lax.Precision.HIGHEST
ridge_weight = 1.0
PIVOT = 128
GROUP = 8
VMEM_BYTES = 56 * 1024 * 1024


def pieces(x, count):
    out = []
    for _ in range(count):
        part = x.astype(BF16)
        out.append(part)
        x = x - part.astype(F32)
    return out


def dot(a, b, dims=((1,), (0,)), precision=None):
    return lax.dot_general(a, b, (dims, ((), ())), precision=precision, preferred_element_type=F32)


def dot3(a, b, dims=((1,), (0,))):
    a0, a1 = pieces(a, 2)
    b0, b1 = pieces(b, 2)
    return dot(a0, b0, dims) + (dot(a0, b1, dims) + dot(a1, b0, dims))


def picked_points(index_col, points, base):
    local = index_col - base
    hot = (lax.broadcasted_iota(jnp.int32, (index_col.shape[0], points.shape[0]), 1) == local).astype(BF16)
    total = None
    for part in reversed(pieces(points, 3)):
        term = dot(hot, part)
        total = term if total is None else total + term
    return total


def picked_resid(index_row, residual, base):
    local = index_row - base
    hot = (lax.broadcasted_iota(jnp.int32, (residual.shape[1], index_row.shape[1]), 0) == local).astype(BF16)
    rows = residual.shape[0]
    got = dot(jnp.concatenate(pieces(residual, 3), axis=0), hot)
    return (got[2 * rows :] + got[rows : 2 * rows]) + got[:rows]


def square_sums(points):
    squares = points * points
    sums = jnp.sum(squares.reshape(points.shape[0] // 8, 8, points.shape[1]), axis=0)
    total = sums[:, :128]
    for start in range(128, points.shape[1], 128):
        total = total + sums[:, start : start + 128]
    return total


def exchange_kernel(dp, mp, index_row, points, residual, out_points, out_resid, out_squares,
                    send, landed, share, full, squares, first_send, first_recv, square_send, square_recv,
                    second_send, second_recv, third_send, third_recv):
    me = lax.axis_index("dp")
    col = lax.axis_index("mp")
    block = index_row.shape[1]
    feat = points.shape[1]
    quarter = block // mp
    rows = quarter // dp
    out_rows = residual.shape[0]
    base = me * points.shape[0]

    barrier = pltpu.get_barrier_semaphore()
    for step in range(1, dp):
        pl.semaphore_signal(barrier, inc=1, device_id=(lax.rem(me + step, dp), col), device_id_type=MESH)
    near, far = col + 1 - 2 * lax.rem(col, 2), lax.rem(col + 2, mp)
    for other in (near, far):
        pl.semaphore_signal(barrier, inc=1, device_id=(me, other), device_id_type=MESH)

    squares[me] = square_sums(points[...])
    own = index_row[:, pl.ds(pl.multiple_of(col * quarter, quarter), quarter)]
    own = jnp.transpose(jnp.broadcast_to(own, (128, quarter)))[:, :1]
    got = picked_points(own, points[...], base)
    resid = picked_resid(index_row[...], residual[...], base)
    for d in range(dp):
        send[d, :, :feat] = got[d * rows : (d + 1) * rows]
        tile, start = divmod(d * rows, out_rows)
        send[d, :, feat:] = resid[start : start + rows, tile * 128 : (tile + 1) * 128]
    pl.semaphore_wait(barrier, dp - 1 + 2)

    first, norms = [], []
    for step in range(1, dp):
        peer = lax.rem(me + step, dp)
        first.append(pltpu.make_async_remote_copy(
            src_ref=send.at[peer], dst_ref=landed.at[me], send_sem=first_send.at[step], recv_sem=first_recv.at[step],
            device_id=(peer, col), device_id_type=MESH))
        first[-1].start()
        norms.append(pltpu.make_async_remote_copy(
            src_ref=squares.at[me], dst_ref=squares.at[me], send_sem=square_send.at[step],
            recv_sem=square_recv.at[step], device_id=(peer, col), device_id_type=MESH))
        norms[-1].start()
    landed[me] = send[me]
    for copy in first:
        copy.wait()
    total = landed[0]
    for d in range(1, dp):
        total = total + landed[d]
    share[...] = total
    second = []
    for step in range(1, dp):
        peer = lax.rem(me + step, dp)
        second.append(pltpu.make_async_remote_copy(
            src_ref=share, dst_ref=full.at[me], send_sem=second_send.at[step], recv_sem=second_recv.at[step],
            device_id=(peer, col), device_id_type=MESH))
        second[-1].start()
    full[me] = total
    third = []
    for step in range(dp):
        source = lax.rem(me + dp - step, dp)
        if step > 0:
            second[step - 1].wait_recv()
        place = pl.ds(pl.multiple_of(col * quarter + source * rows, rows), rows)
        out_points[place, :] = full[source, :, :feat]
        for kind, other in enumerate((far, near)):
            third.append(pltpu.make_async_remote_copy(
                src_ref=full.at[source, :, pl.ds(0, feat)], dst_ref=out_points.at[place, :],
                send_sem=third_send.at[step, kind], recv_sem=third_recv.at[step, kind],
                device_id=(me, other), device_id_type=MESH))
            third[-1].start()
    fourth = []
    for step in range(dp):
        source = lax.rem(me + dp - step, dp)
        third[2 * step].wait_recv()
        place = pl.ds(pl.multiple_of(far * quarter + source * rows, rows), rows)
        fourth.append(pltpu.make_async_remote_copy(
            src_ref=out_points.at[place, :], dst_ref=out_points.at[place, :],
            send_sem=third_send.at[step, 2], recv_sem=third_recv.at[step, 2],
            device_id=(me, near), device_id_type=MESH))
        fourth[-1].start()
    for copy in norms:
        copy.wait()
    sums = squares[0]
    for d in range(1, dp):
        sums = sums + squares[d]
    out_squares[...] = sums
    for d in range(dp):
        tile, start = divmod(d * rows, out_rows)
        out_resid[start : start + rows, tile * 128 : (tile + 1) * 128] = full[d, :, feat:]
    for copy in second:
        copy.wait_send()
    for step in range(dp):
        third[2 * step].wait_send()
        third[2 * step + 1].wait()
        fourth[step].wait()


def exchange(dp, mp, index_row, points, residual):
    block, feat = index_row.shape[1], points.shape[1]
    rows = block // (dp * mp)
    out_rows = residual.shape[0]
    width = feat + 128
    vmem = pl.BlockSpec(memory_space=pltpu.VMEM)
    dma = pltpu.SemaphoreType.DMA
    return pl.pallas_call(
        functools.partial(exchange_kernel, dp, mp),
        out_shape=(jax.ShapeDtypeStruct((block, feat), F32), jax.ShapeDtypeStruct((out_rows, block), F32),
                   jax.ShapeDtypeStruct((8, 128), F32)),
        in_specs=[vmem] * 3,
        out_specs=(vmem,) * 3,
        scratch_shapes=[
            pltpu.VMEM((dp, rows, width), F32), pltpu.VMEM((dp, rows, width), F32), pltpu.VMEM((rows, width), F32),
            pltpu.VMEM((dp, rows, width), F32), pltpu.VMEM((dp, 8, 128), F32),
            dma((dp,)), dma((dp,)), dma((dp,)), dma((dp,)), dma((dp,)), dma((dp,)), dma((dp, 3)), dma((dp, 3)),
        ],
        compiler_params=pltpu.CompilerParams(collective_id=0, has_side_effects=True, vmem_limit_bytes=VMEM_BYTES),
    )(index_row, points, residual)


def exchange_by_sums(dp, mp, index_row, points, residual):
    base = lax.axis_index("dp") * points.shape[0]
    local = index_row[0] - base
    mine = (local >= 0) & (local < points.shape[0])
    safe = jnp.where(mine, local, 0)
    got = jnp.where(mine[:, None], points[safe], 0.0)
    resid = jnp.where(mine[None, :], residual[:, safe], 0.0)
    return tuple(lax.psum(x, "dp") for x in (got, resid, square_sums(points)))


def invert(matrix, beside):
    size = matrix.shape[0]
    lane = lax.broadcasted_iota(jnp.int32, (size, size), 1)
    lane_group = lax.broadcasted_iota(jnp.int32, (GROUP, size), 1)
    row_group = lax.broadcasted_iota(jnp.int32, (GROUP, size), 0)
    for start in range(0, size, GROUP):
        stop = start + GROUP
        small = [jnp.broadcast_to(matrix[start:stop, j : j + 1], (GROUP, size)) for j in range(start, stop)]
        own = jnp.where(lane_group < start, -matrix[start:stop], matrix[start:stop])
        c0, c1, c2 = [p.astype(F32) for p in pieces(own, 3)]
        side = jnp.concatenate([c0, c0, c0, c1, c1, c2], axis=0).astype(BF16)
        panel = jnp.where((lane_group >= start) & (lane_group < stop),
                          (lane_group - start == row_group).astype(F32), matrix[start:stop])
        for j in range(0, GROUP, 2):
            k = j + 1
            on_j, on_k = row_group == j, row_group == k
            p, q, r = small[j][j : j + 1], small[j][k : k + 1], small[k][k : k + 1]
            scale = 1.0 / (p * r - q * q)
            low, cross, high = r * scale, q * scale, p * scale
            left = jnp.where(on_j, -1.0, jnp.where(on_k, 0.0, small[j]))
            right = jnp.where(on_k, -1.0, jnp.where(on_j, 0.0, small[k]))
            pivots = on_j | on_k

            def reduced(x):
                x0, x1 = x[j : j + 1], x[k : k + 1]
                y0, y1 = x0 * low - x1 * cross, x1 * high - x0 * cross
                return jnp.where(pivots, 0.0, x) - left * y0 - right * y1

            for l in range(j + 2, GROUP):
                small[l] = reduced(small[l])
            panel = reduced(panel)
        beside(start // GROUP)
        ahead = None
        if stop < size:
            old = matrix[stop : stop + GROUP]
            ahead = jnp.where((lane_group >= start) & (lane_group < stop), 0.0, old)
            for j in range(GROUP):
                ahead = ahead - jnp.broadcast_to(old[:, start + j : start + j + 1], (GROUP, size)) * panel[j : j + 1]
        zeroed = jnp.where((lane >= start) & (lane < stop), 0.0, matrix)
        r0, r1, r2 = [p.astype(F32) for p in pieces(panel, 3)]
        matrix = zeroed - dot(side, jnp.concatenate([r0, r1, r2, r0, r1, r0], axis=0).astype(BF16), ((0,), (0,)))
        parts = [matrix[:start], panel] + ([] if ahead is None else [ahead, matrix[stop + GROUP :]])
        matrix = jnp.concatenate([p for p in parts if p.shape[0]], axis=0)
    return matrix


def step_kernel(examples, index_row, points, residual, coeffs, block_points, block_resid, squares,
                new_residual, new_coeffs, system, weights0, weights1, index_col):
    block, feat = block_points.shape
    count = points.shape[0]
    out_rows = residual.shape[0]
    base = lax.axis_index("dp") * count
    inverse_mean = examples / jnp.sum(squares[...])
    ones = jnp.ones((8, feat), F32)
    centers = block_points[...]
    center_sq = jnp.sum(centers * centers, axis=1, keepdims=True)
    center_sq_row = dot(ones, centers * centers, ((1,), (1,)), HIGHEST)[:1]
    inner = dot(centers, centers, ((1,), (1,)), HIGHEST)
    diagonal = lax.broadcasted_iota(jnp.int32, (block, block), 0) == lax.broadcasted_iota(jnp.int32, (block, block), 1)
    system[:block, :] = (jnp.exp(-(center_sq + center_sq_row - 2.0 * inner) * inverse_mean)
                         + jnp.where(diagonal, ridge_weight, 0.0))
    system[block:, :] = block_resid[...]
    index_col[...] = jnp.transpose(jnp.broadcast_to(index_row[...], (128, block)))

    groups = PIVOT // GROUP
    strips = block // PIVOT
    some_rows = count // (strips * (groups // strips))
    lane = lax.broadcasted_iota(jnp.int32, (PIVOT, block), 1)
    lane_all = lax.broadcasted_iota(jnp.int32, (block + out_rows, block), 1)

    @pl.loop(0, strips)
    def _(step):
        here = pl.ds(pl.multiple_of(step * PIVOT, PIVOT), PIVOT)
        held = {}

        def beside(n):
            strip = n % strips
            first = step * (groups // strips) + n // strips
            there = pl.ds(pl.multiple_of(first * some_rows, some_rows), some_rows)
            some = points[there, :]
            if strip == 0:
                held["sq"] = dot(ones, some * some, ((1,), (1,)), HIGHEST)[:1]
            rows = slice(strip * PIVOT, (strip + 1) * PIVOT)
            inner = dot(block_points[rows, :], some, ((1,), (1,)), HIGHEST)
            weights = jnp.exp(-(center_sq[rows] + held["sq"] - 2.0 * inner) * inverse_mean)
            w0, w1 = pieces(weights, 2)
            weights0[rows, there] = w0
            weights1[rows, there] = w1

        inverse = invert(system[here, here], beside)
        inside = (lane >= step * PIVOT) & (lane < (step + 1) * PIVOT)
        scaled = dot(inverse, system[here, :], precision=HIGHEST)
        scaled = jnp.where(inside, -jnp.concatenate([inverse] * strips, axis=1), scaled)
        left = system[:, here]
        inside_all = (lane_all >= step * PIVOT) & (lane_all < (step + 1) * PIVOT)
        system[...] = jnp.where(inside_all, 0.0, system[...]) - dot(left, scaled, precision=HIGHEST)

    high, mid, low = pieces(system[block:, :], 3)
    stack3 = jnp.concatenate([high, mid, low], axis=0)
    stack2 = jnp.concatenate([high, mid], axis=0)
    tile = 512

    @pl.loop(0, count // tile)
    def _(i):
        here = pl.ds(pl.multiple_of(i * tile, tile), tile)
        main = dot(stack2, weights0[:, here])
        change = main[:out_rows] + (main[out_rows:] + dot(high, weights1[:, here]))
        local = jnp.concatenate([index_col[...]] * (tile // 128), axis=1) - (base + i * tile)
        hot = (lax.broadcasted_iota(jnp.int32, (block, tile), 1) == local).astype(BF16)
        placed = dot(stack3, hot)
        added = (placed[2 * out_rows :] + placed[out_rows : 2 * out_rows]) + placed[:out_rows]
        new_residual[:, here] = (residual[:, here] - change) - ridge_weight * added
        new_coeffs[:, here] = coeffs[:, here] + added


def step(examples, index_row, points, residual, coeffs, block_points, block_resid, squares):
    block = block_points.shape[0]
    vmem = pl.BlockSpec(memory_space=pltpu.VMEM)
    return pl.pallas_call(
        functools.partial(step_kernel, examples),
        out_shape=(jax.ShapeDtypeStruct(residual.shape, F32), jax.ShapeDtypeStruct(coeffs.shape, F32)),
        in_specs=[vmem] * 7,
        out_specs=(vmem,) * 2,
        scratch_shapes=[pltpu.VMEM((block + residual.shape[0], block), F32),
                        pltpu.VMEM((block, points.shape[0]), BF16), pltpu.VMEM((block, points.shape[0]), BF16),
                        pltpu.VMEM((block, 128), jnp.int32)],
        compiler_params=pltpu.CompilerParams(vmem_limit_bytes=VMEM_BYTES),
    )(index_row, points, residual, coeffs, block_points, block_resid, squares)


def solution(mesh):
    dp, mp = mesh.shape["dp"], mesh.shape["mp"]

    def on_device(points, residual, coeffs, block_index):
        index_row = block_index[None, :]
        block, out_rows = block_index.shape[0], residual.shape[0]
        rows = block // (dp * mp)
        fits = mp == 4 and block // mp == 128 and rows % 8 == 0 and out_rows % rows == 0 and rows * dp * mp == block and out_rows * block == dp * rows * 128
        gathered = (exchange if fits else exchange_by_sums)(dp, mp, index_row, points, residual)
        return step(points.shape[0] * dp, index_row, points, residual, coeffs, *gathered)

    return jax.shard_map(
        on_device,
        mesh=mesh,
        in_specs=(P("dp", None), P("mp", "dp"), P("mp", "dp"), P()),
        out_specs=(P("mp", "dp"), P("mp", "dp")),
        check_vma=False,
    )
```
